256 devices in a mesh: dp: 32 (over y_hi, z, core), blk: 4 (over x), uly: 2 (over y_lo).
Axes of the slice: x: 4, y: 4 (y_hi: 2, y_lo: 2; y = y_hi * 2 + y_lo), z: 8, core: 2. Of those that a mesh axis runs over, the one named last changes fastest.
Arguments:
- img_query: bfloat16 [32, 1024, 2432], P('dp', ('blk', 'uly')), may hold values from -6 to 6
- img_key: bfloat16 [32, 1024, 2432], P('dp', ('blk', 'uly')), may hold values from -6 to 6
- img_value: bfloat16 [32, 1024, 2432], P('dp', ('blk', 'uly')), may hold values from -6 to 6
- img_cotangent: bfloat16 [32, 1024, 2432], P('dp', ('blk', 'uly')), may hold values from -6 to 6
- txt_query: bfloat16 [32, 32, 2432], P('dp', None, 'uly'), may hold values from -6 to 6
- txt_key: bfloat16 [32, 32, 2432], P('dp', None, 'uly'), may hold values from -6 to 6
- txt_value: bfloat16 [32, 32, 2432], P('dp', None, 'uly'), may hold values from -6 to 6
- txt_cotangent: bfloat16 [32, 32, 2432], P('dp', None, 'uly'), may hold values from -6 to 6
- img_gate: bfloat16 [32, 2432], P('dp'), may hold values from -6 to 6
- txt_gate: bfloat16 [32, 2432], P('dp'), may hold values from -6 to 6
- conditioning: bfloat16 [32, 2432], P('dp'), may hold values from -6 to 6
- norm_gains: float32 [4, 64], replicated, may hold values from 0.1 to 1.9
Outputs:
- img_query_grad: bfloat16 [32, 1024, 2432], P('dp', ('blk', 'uly'))
- img_key_grad: bfloat16 [32, 1024, 2432], P('dp', ('blk', 'uly'))
- img_value_grad: bfloat16 [32, 1024, 2432], P('dp', ('blk', 'uly'))
- txt_query_grad: bfloat16 [32, 32, 2432], P('dp', None, 'uly')
- txt_key_grad: bfloat16 [32, 32, 2432], P('dp', None, 'uly')
- txt_value_grad: bfloat16 [32, 32, 2432], P('dp', None, 'uly')
- modulation_grad: float32 [2432, 2432], P('blk', 'uly')
- txt_gate_grad: float32 [32, 2432], P('dp', 'uly')
The draws below stay inside these ranges and needn't reach their ends.
All inputs are finite; a program needn't handle non-finite values.
Results may differ from the reference program's by a relative error of at most 0.025.
Values may be sent and summed in bfloat16 or wider, within the bound.
No kernel may reach another device: no remote copies, remote signals or barrier semaphores. Data moves between devices by JAX's collectives and lax.ppermute only.
A program may use at most 192 MiB of HBM per device.

```python
import math
import jax
import jax.numpy as jnp
from jax import lax

HEADS = 38
HEAD = 64
D = 2432
TXT = 32
IMG = 1024
SAMPLES = 32


def levels(rng, extent, cuts, smallest, top_value):
    factor_of, own = 1.0, jax.random.fold_in(rng, 6)
    for position, parts in cuts:
        draws = jnp.exp(jax.random.uniform(jax.random.fold_in(own, position), (parts,), jnp.float32, smallest / len(cuts), top_value / len(cuts)))
        factor_of = factor_of * jnp.repeat(draws, extent[position] // parts).reshape([-1 if axis == position else 1 for axis in range(len(extent))])
    return factor_of


def scatter_about(own_key, dims, scale, most, shards=(), held_as=jnp.bfloat16):
    loudness = levels(own_key, dims, shards, -0.22, 0.18) if shards else 1.0
    result = jax.random.normal(own_key, dims, jnp.float32) * scale * loudness
    return jnp.minimum(jnp.maximum(result, -most), most).astype(held_as)


def setup_inputs(seed: int = 0) -> dict:
    key_list = jax.random.split(jax.random.key(seed), 13)
    img_query = scatter_about(key_list[0], (SAMPLES, IMG, D), 1.0, 6.0, ((0, 32), (1, 8)))
    img_key = scatter_about(key_list[1], (SAMPLES, IMG, D), 1.0, 6.0, ((0, 32), (1, 8)))
    img_value = scatter_about(key_list[2], (SAMPLES, IMG, D), 1.0, 6.0, ((0, 32), (1, 8)))
    img_cotangent = scatter_about(key_list[3], (SAMPLES, IMG, D), 1.0, 6.0, ((0, 32), (1, 8)))
    txt_query = scatter_about(key_list[4], (SAMPLES, TXT, D), 1.0, 6.0, ((0, 32), (2, 2)))
    txt_key = scatter_about(key_list[5], (SAMPLES, TXT, D), 1.0, 6.0, ((0, 32), (2, 2)))
    txt_value = scatter_about(key_list[6], (SAMPLES, TXT, D), 1.0, 6.0, ((0, 32), (2, 2)))
    txt_cotangent = scatter_about(key_list[7], (SAMPLES, TXT, D), 1.0, 6.0, ((0, 32), (2, 2)))
    img_gate = scatter_about(key_list[8], (SAMPLES, D), 1.0, 6.0, ((0, 32),))
    txt_gate = scatter_about(key_list[9], (SAMPLES, D), 1.0, 6.0, ((0, 32),))
    conditioning = scatter_about(key_list[10], (SAMPLES, D), 1.0, 6.0, ((0, 32),))
    norm_gains = jnp.clip(1.0 + 0.18 * jax.random.normal(key_list[11], (4, HEAD), jnp.float32), 0.1, 1.9)
    return dict(img_query=img_query, img_key=img_key, img_value=img_value, img_cotangent=img_cotangent, txt_query=txt_query, txt_key=txt_key, txt_value=txt_value, txt_cotangent=txt_cotangent, img_gate=img_gate, txt_gate=txt_gate, conditioning=conditioning, norm_gains=norm_gains)


EPS = 1e-06

def normalize(values_in, gain):
    widened = values_in.astype(jnp.float32)
    inverse = lax.rsqrt(lax.optimization_barrier(jnp.mean(widened * widened, -1, keepdims=True)) + EPS)
    return (widened * inverse * gain, widened, inverse)

def norm_back(widened, inverse, gain, upstream):
    scaled = upstream * gain
    return inverse * scaled - widened * inverse ** 3 * lax.optimization_barrier(jnp.mean(widened * scaled, -1, keepdims=True))

def attend_forward(queries, keys_in, values_in, score_scale):
    scores = jnp.einsum('qhe,khe->hqk', queries.astype(jnp.float32), keys_in.astype(jnp.float32)) * score_scale
    exponent = jnp.exp(scores)
    totals = lax.optimization_barrier(jnp.sum(exponent, -1))
    weighted = jnp.einsum('hqk,khe->qhe', exponent.astype(jnp.bfloat16).astype(jnp.float32), values_in.astype(jnp.float32))
    return (totals, weighted)

def attend_back(queries, upstream, totals, row_delta, keys_in, values_in, score_scale):
    scores = jnp.einsum('qhe,khe->hqk', queries.astype(jnp.float32), keys_in.astype(jnp.float32)) * score_scale
    probability = jnp.exp(scores) / totals[:, :, None]
    prob_grad = jnp.einsum('qhe,khe->hqk', upstream.astype(jnp.float32), values_in.astype(jnp.float32))
    score_grad = (probability * (prob_grad - row_delta.T[:, :, None])).astype(jnp.bfloat16).astype(jnp.float32)
    query_grad = jnp.einsum('hqk,khe->qhe', score_grad, keys_in.astype(jnp.float32)) * score_scale
    key_grad = jnp.einsum('hqk,qhe->khe', score_grad, queries.astype(jnp.float32)) * score_scale
    value_grad = jnp.einsum('hqk,qhe->khe', probability.astype(jnp.bfloat16).astype(jnp.float32), upstream.astype(jnp.float32))
    return (query_grad, key_grad, value_grad)

def reference(img_query, img_key, img_value, img_cotangent, txt_query, txt_key, txt_value, txt_cotangent, img_gate, txt_gate, conditioning, norm_gains):
    score_scale = 1.0 / math.sqrt(HEAD)

    def split_heads(matrix):
        return matrix.reshape(matrix.shape[0], HEADS, HEAD)

    def one_sample(inputs):
        iq, ik, iv, icot, tq, tk, tv, tcot, igate, tgate = inputs
        iq_norm, iq_wide, iq_inv = normalize(split_heads(iq), norm_gains[0])
        ik_norm, ik_wide, ik_inv = normalize(split_heads(ik), norm_gains[1])
        tq_norm, tq_wide, tq_inv = normalize(split_heads(tq), norm_gains[2])
        tk_norm, tk_wide, tk_inv = normalize(split_heads(tk), norm_gains[3])
        queries = jnp.concatenate([tq_norm, iq_norm], 0).astype(jnp.bfloat16)
        keys_all = jnp.concatenate([tk_norm, ik_norm], 0).astype(jnp.bfloat16)
        values_all = jnp.concatenate([split_heads(tv), split_heads(iv)], 0)
        totals, weighted = attend_forward(queries, keys_all, values_all, score_scale)
        attention = (weighted / totals.T[:, :, None]).astype(jnp.bfloat16)
        gated = jnp.concatenate([tcot.astype(jnp.float32) * tgate.astype(jnp.float32), icot.astype(jnp.float32) * igate.astype(jnp.float32)], 0)
        upstream = split_heads(gated.astype(jnp.bfloat16))
        row_delta = lax.optimization_barrier(jnp.sum(upstream.astype(jnp.float32) * attention.astype(jnp.float32), -1))
        query_grad, key_grad, value_grad = attend_back(queries, upstream, totals, row_delta, keys_all, values_all, score_scale)
        rows_txt = tq.shape[0]
        flat_attn = attention.reshape(attention.shape[0], HEADS * HEAD).astype(jnp.float32)
        tq_grad = norm_back(tq_wide, tq_inv, norm_gains[2], query_grad[:rows_txt]).astype(jnp.bfloat16)
        iq_grad = norm_back(iq_wide, iq_inv, norm_gains[0], query_grad[rows_txt:]).astype(jnp.bfloat16)
        tk_grad = norm_back(tk_wide, tk_inv, norm_gains[3], key_grad[:rows_txt]).astype(jnp.bfloat16)
        ik_grad = norm_back(ik_wide, ik_inv, norm_gains[1], key_grad[rows_txt:]).astype(jnp.bfloat16)
        value_out = value_grad.astype(jnp.bfloat16)
        gate_img = lax.optimization_barrier(jnp.sum(icot.astype(jnp.float32) * flat_attn[rows_txt:], 0))
        gate_txt = lax.optimization_barrier(jnp.sum(tcot.astype(jnp.float32) * flat_attn[:rows_txt], 0))
        width = HEADS * HEAD
        return (iq_grad.reshape(-1, width), ik_grad.reshape(-1, width), value_out[rows_txt:].reshape(-1, width), tq_grad.reshape(-1, width), tk_grad.reshape(-1, width), value_out[:rows_txt].reshape(-1, width), gate_img, gate_txt)
    results = lax.map(one_sample, (img_query, img_key, img_value, img_cotangent, txt_query, txt_key, txt_value, txt_cotangent, img_gate, txt_gate))
    iq_out, ik_out, iv_out, tq_out, tk_out, tv_out, gate_img_grad, gate_txt_grad = results
    modulation_grad = jnp.dot(conditioning.astype(jnp.float32).T, gate_img_grad, precision=lax.Precision.HIGHEST)
    return (iq_out, ik_out, iv_out, tq_out, tk_out, tv_out, modulation_grad, gate_txt_grad)
```

```python
import functools

import jax
import jax.numpy as jnp
from jax import lax
from jax.experimental import pallas as pl
from jax.experimental.pallas import tpu as pltpu
from jax.sharding import PartitionSpec as P

HEAD = 64
PAIR = 2 * HEAD
EPS = 1e-06
SLOTS = 5
QUERY_STEPS = 3
TEXT_ROWS = 48
GATE_ROW = SLOTS * TEXT_ROWS
VMEM = 56 * 2**20
f32 = jnp.float32
bf16 = jnp.bfloat16


def head_of(dest, slot, half_heads):
    place = (dest // 2) * SLOTS + slot
    return (dest % 2) * half_heads + place if place < half_heads else None


def matmul(left, right):
    return jnp.dot(left, right, preferred_element_type=f32)


def matmul_nt(left, right):
    return lax.dot_general(left, right, (((1,), (1,)), ((), ())), preferred_element_type=f32)


def split_two(wide):
    high = wide.astype(bf16)
    return high, (wide - high.astype(f32)).astype(bf16)


def split_three(wide):
    high = wide.astype(bf16)
    rest = wide - high.astype(f32)
    middle = rest.astype(bf16)
    return high, middle, (rest - middle.astype(f32)).astype(bf16)


def half_means(wide, averager):
    return matmul(jnp.concatenate(split_two(wide), 1), averager)


def pack_kernel(
    half_heads,
    chunks,
    place_ref,
    iq_ref,
    ik_ref,
    iv_ref,
    ic_ref,
    tq_ref,
    tk_ref,
    tv_ref,
    tc_ref,
    ig_ref,
    tg_ref,
    *out_refs,
):
    send_refs, (text_ref, gate_ref) = out_refs[:-2], out_refs[-2:]

    def columns(ref, head):
        return ref[:, head * HEAD : (head + 1) * HEAD]

    rows = iq_ref.shape[0]
    for slots, send_ref in zip(chunks, send_refs):
        for dest in range(send_ref.shape[0]):
            for position, slot in enumerate(slots):
                head = head_of(dest, slot, half_heads)
                for pair, (first, second) in enumerate(((iq_ref, ik_ref), (iv_ref, ic_ref))):
                    tile = (
                        jnp.zeros((rows, PAIR), bf16)
                        if head is None
                        else jnp.concatenate([columns(first, head), columns(second, head)], 1)
                    )
                    start = (2 * position + pair) * rows
                    send_ref[dest, start : start + rows, :] = tile
    place = place_ref[0]
    for device in range(send_refs[0].shape[0]):

        @pl.when(place == device)
        def _():
            for slot in range(SLOTS):
                head = head_of(device, slot, half_heads)
                local = None if head is None else head - (device % 2) * half_heads
                for pair, (first, second) in enumerate(((tq_ref, tk_ref), (tv_ref, tc_ref))):
                    tile = (
                        jnp.zeros((first.shape[0], PAIR), bf16)
                        if local is None
                        else jnp.concatenate([columns(first, local), columns(second, local)], 1)
                    )
                    text_ref[:, (2 * slot + pair) * PAIR : (2 * slot + pair + 1) * PAIR] = tile
                for row, ref in enumerate((ig_ref, tg_ref)):
                    gate = jnp.zeros((1, HEAD), bf16) if head is None else columns(ref, head)
                    gate = gate.astype(f32)
                    gate_ref[slot, row : row + 1, :] = jnp.concatenate([gate, gate], 1)


def attend_kernel(count, in_ref, text_ref, gain_ref, gate_ref, out_ref, pay_ref, sums_ref):
    step = pl.program_id(0)
    devices, tile_rows = in_ref.shape[0], in_ref.shape[1] // 2
    rows, txt = devices * tile_rows, text_ref.shape[0]
    total_rows = rows + txt
    row_at = lax.broadcasted_iota(jnp.int32, (2 * PAIR, PAIR), 0)
    lane_at = lax.broadcasted_iota(jnp.int32, (2 * PAIR, PAIR), 1)
    averager = jnp.where((row_at % PAIR) // HEAD == lane_at // HEAD, 1.0 / HEAD, 0.0).astype(bf16)

    raw = jnp.concatenate(
        [in_ref[:, :tile_rows, :].reshape(rows, PAIR), text_ref[:, :PAIR]], 0
    ).astype(f32)
    value_cotan = jnp.concatenate(
        [in_ref[:, tile_rows:, :].reshape(rows, PAIR), text_ref[:, PAIR:]], 0
    )
    gain = jnp.concatenate(
        [
            jnp.broadcast_to(gain_ref[0:1, :], (rows, PAIR)),
            jnp.broadcast_to(gain_ref[1:2, :], (txt, PAIR)),
        ],
        0,
    )
    inverse = lax.rsqrt(half_means(raw * raw, averager) + EPS)
    normed = (raw * inverse * gain).astype(bf16)
    queries, keys = normed[:, :HEAD], normed[:, HEAD:]
    scaled_queries = queries * jnp.asarray(0.125, bf16)
    values_ones = jnp.concatenate([value_cotan[:, :HEAD], jnp.ones((total_rows, HEAD), bf16)], 1)
    keys_zeros = jnp.concatenate([keys, jnp.zeros((total_rows, HEAD), bf16)], 1)
    cotan = value_cotan[:, HEAD:].astype(f32)
    gate = jnp.concatenate(
        [
            jnp.broadcast_to(gate_ref[0, 0:1, :HEAD], (rows, HEAD)),
            jnp.broadcast_to(gate_ref[0, 1:2, :HEAD], (txt, HEAD)),
        ],
        0,
    )
    upstream = (cotan * gate).astype(bf16).astype(f32)

    size = total_rows // QUERY_STEPS
    lane = lax.broadcasted_iota(jnp.int32, (size, PAIR), 1)
    ones = jnp.ones((2 * HEAD, PAIR), bf16)
    zeros = jnp.zeros((size, HEAD), bf16)
    query_grads = []
    value_key_grad = img_sum = txt_sum = None
    for part in range(QUERY_STEPS):
        at = slice(part * size, (part + 1) * size)
        exponent = jnp.exp(matmul_nt(scaled_queries[at], keys)).astype(bf16)
        weighted = matmul(exponent, values_ones)
        over_total = 1.0 / weighted[:, HEAD:]
        attention = (weighted[:, :HEAD] * over_total).astype(bf16).astype(f32)
        scaled = (upstream[at] * over_total).astype(bf16)
        delta = matmul(jnp.concatenate(split_two(scaled.astype(f32) * attention), 1), ones)
        delta_high, delta_low = split_two(delta)
        extended = jnp.where(
            lane < HEAD,
            jnp.concatenate([scaled, zeros], 1),
            jnp.where(
                lane == HEAD,
                -delta_high,
                jnp.where(lane == HEAD + 1, -delta_low, jnp.zeros_like(delta_low)),
            ),
        )
        prob_grad = matmul_nt(extended, values_ones)
        score_grad = exponent * prob_grad.astype(bf16)
        query_grads.append(matmul(score_grad, keys_zeros))
        term = jnp.concatenate(
            [matmul(scaled.T, exponent), matmul(queries[at].T, score_grad)], 0
        )
        value_key_grad = term if value_key_grad is None else value_key_grad + term
        gated = cotan[at] * attention
        img_rows = min(max(rows - part * size, 0), size)
        if img_rows > 0:
            term = jnp.sum(gated[:img_rows], 0, keepdims=True)
            img_sum = term if img_sum is None else img_sum + term
        if img_rows < size:
            term = jnp.sum(gated[img_rows:], 0, keepdims=True)
            txt_sum = term if txt_sum is None else txt_sum + term
    value_key_grad = value_key_grad.T
    lane = lax.broadcasted_iota(jnp.int32, (total_rows, PAIR), 1)
    scaled = jnp.where(lane < HEAD, jnp.concatenate(query_grads, 0), value_key_grad) * (gain * 0.125)
    mean = half_means(raw * scaled, averager)
    pair_grad = (inverse * scaled - raw * (inverse * inverse * inverse) * mean).astype(bf16)
    value_grad = value_key_grad[:, :HEAD].astype(bf16)

    start = pl.multiple_of(step * tile_rows, tile_rows)
    out_ref[:, pl.ds(start, tile_rows), :] = pair_grad[:rows].reshape(devices, tile_rows, PAIR)
    tiled = value_grad[:rows].reshape(devices, tile_rows, HEAD)
    half = tile_rows // 2
    for head in range(count):

        @pl.when(step == head)
        def _():
            begin = (count + head // 2) * tile_rows
            if head % 2 == 1:
                out_ref[:, begin : begin + tile_rows, HEAD:] = tiled
            elif head < count - 1:
                out_ref[:, begin : begin + tile_rows, :HEAD] = tiled
            else:
                out_ref[:, begin : begin + half, :] = jnp.concatenate(
                    [tiled[:, :half], tiled[:, half:]], 2
                )

    text_grad = value_grad[rows:]
    text_tile = jnp.concatenate(
        [pair_grad[rows:], jnp.concatenate([text_grad[: txt // 2], text_grad[txt // 2 :]], 1)], 0
    )
    start = pl.multiple_of(step * TEXT_ROWS, 16)
    for dest in range(pay_ref.shape[0]):
        pay_ref[dest, pl.ds(start, TEXT_ROWS), :] = text_tile
    sums_ref[pl.ds(step, 1), :] = jnp.concatenate([img_sum, txt_sum], 1)

    @pl.when(step == count - 1)
    def _():
        sums = sums_ref[0:SLOTS, :]
        tail = pay_ref.shape[1] - GATE_ROW - 3 * SLOTS
        packed = jnp.concatenate(
            [part.astype(f32) for part in split_three(sums)] + [jnp.zeros((tail, PAIR), f32)], 0
        ).astype(bf16)
        for dest in range(pay_ref.shape[0]):
            pay_ref[dest, GATE_ROW:, :] = packed


def text_kernel(half_heads, pay_ref, tq_ref, tk_ref, tv_ref, tg_ref, row_ref):
    txt = tq_ref.shape[0]
    blocks = pay_ref.shape[0]
    for block in range(blocks):
        packed = pay_ref[block, GATE_ROW:, :].astype(f32)
        sums = packed[:SLOTS] + packed[SLOTS : 2 * SLOTS] + packed[2 * SLOTS : 3 * SLOTS]
        for slot in range(SLOTS):
            head = block * SLOTS + slot
            if head >= half_heads:
                continue
            lanes = slice(head * HEAD, (head + 1) * HEAD)
            base = slot * TEXT_ROWS
            pair = pay_ref[block, base : base + txt, :]
            folded = pay_ref[block, base + txt : base + TEXT_ROWS, :]
            tq_ref[:, lanes] = pair[:, :HEAD]
            tk_ref[:, lanes] = pair[:, HEAD:]
            tv_ref[:, lanes] = jnp.concatenate([folded[:, :HEAD], folded[:, HEAD:]], 0)
            tg_ref[:, lanes] = sums[slot : slot + 1, HEAD:]
            for dest in range(row_ref.shape[0]):
                row_ref[dest, :, lanes] = sums[slot : slot + 1, :HEAD]


def modulation_kernel(cond_ref, gate_ref, out_ref):
    cond = cond_ref[...]
    gates = jnp.concatenate(split_three(gate_ref[...]), 0)
    out_ref[...] = lax.dot_general(
        jnp.concatenate([cond, cond, cond], 0),
        gates,
        (((0,), (0,)), ((), ())),
        preferred_element_type=f32,
    )


def unpack_kernel(half_heads, chunks, *refs):
    back_refs, (q_ref, k_ref, v_ref) = refs[:-3], refs[-3:]
    rows = q_ref.shape[0]
    half = rows // 2
    pieces = {}
    for slots, back_ref in zip(chunks, back_refs):
        count = len(slots)
        for source in range(back_ref.shape[0]):
            for position, slot in enumerate(slots):
                head = head_of(source, slot, half_heads)
                if head is None:
                    continue
                begin = (count + position // 2) * rows
                if position % 2 == 1:
                    value = back_ref[source, begin : begin + rows, HEAD:]
                elif position < count - 1:
                    value = back_ref[source, begin : begin + rows, :HEAD]
                else:
                    folded = back_ref[source, begin : begin + half, :]
                    value = jnp.concatenate([folded[:, :HEAD], folded[:, HEAD:]], 0)
                pair = back_ref[source, position * rows : (position + 1) * rows, :]
                pieces[head] = (pair[:, :HEAD], pair[:, HEAD:], value)
    for head in range(0, 2 * half_heads, 2):
        lanes = slice(head * HEAD, (head + 2) * HEAD)
        for which, ref in enumerate((q_ref, k_ref, v_ref)):
            ref[:, lanes] = jnp.concatenate([pieces[head][which], pieces[head + 1][which]], 1)


def shards(
    img_query,
    img_key,
    img_value,
    img_cotangent,
    txt_query,
    txt_key,
    txt_value,
    txt_cotangent,
    img_gate,
    txt_gate,
    conditioning,
    norm_gains,
):
    _, rows, width = img_query.shape
    _, txt, half_width = txt_query.shape
    half_heads = half_width // HEAD
    blocks, halves, samples = lax.axis_size("blk"), lax.axis_size("uly"), lax.axis_size("dp")
    devices = blocks * halves
    chunks = (tuple(range(SLOTS)),)
    params = pltpu.CompilerParams(vmem_limit_bytes=VMEM)
    place = lax.axis_index("blk") * halves + lax.axis_index("uly")

    vmem = pl.BlockSpec(memory_space=pltpu.VMEM)
    packed = pl.pallas_call(
        functools.partial(pack_kernel, half_heads, chunks),
        in_specs=[pl.BlockSpec(memory_space=pltpu.SMEM)] + [vmem] * 10,
        out_specs=[vmem] * (len(chunks) + 2),
        out_shape=[
            jax.ShapeDtypeStruct((devices, 2 * len(slots) * rows, PAIR), bf16) for slots in chunks
        ]
        + [
            jax.ShapeDtypeStruct((txt, 2 * SLOTS * PAIR), bf16),
            jax.ShapeDtypeStruct((SLOTS, 2, PAIR), f32),
        ],
        compiler_params=params,
        name="pack",
    )(
        place[None],
        img_query[0],
        img_key[0],
        img_value[0],
        img_cotangent[0],
        txt_query[0],
        txt_key[0],
        txt_value[0],
        txt_cotangent[0],
        img_gate,
        txt_gate,
    )
    sends, text_rows, gates = packed[:-2], packed[-2], packed[-1]
    gains = norm_gains.reshape(2, PAIR)

    width_rows = width // blocks
    cond_rows = lax.dynamic_slice_in_dim(
        conditioning, lax.axis_index("blk") * width_rows, width_rows, 1
    )
    cond_all = lax.all_to_all(
        jnp.broadcast_to(cond_rows[None], (samples, 1, width_rows)), "dp", 0, 0, tiled=True
    ).reshape(samples, width_rows)

    received = [lax.all_to_all(send, ("blk", "uly"), 0, 0, tiled=True) for send in sends]
    backs = []
    for slots, arrived in zip(chunks, received):
        count = len(slots)
        out_rows = (2 * count + count) * rows // 2
        back, pay = pl.pallas_call(
            functools.partial(attend_kernel, count),
            grid=(count,),
            in_specs=[
                pl.BlockSpec((devices, 2 * rows, PAIR), lambda h: (0, h, 0)),
                pl.BlockSpec((txt, 2 * PAIR), lambda h: (0, h)),
                pl.BlockSpec((2, PAIR), lambda h: (0, 0)),
                pl.BlockSpec((1, 2, PAIR), lambda h: (h, 0, 0)),
            ],
            out_specs=[
                pl.BlockSpec((devices, out_rows, PAIR), lambda h: (0, 0, 0)),
                pl.BlockSpec((blocks, GATE_ROW + 16, PAIR), lambda h: (0, 0, 0)),
            ],
            out_shape=[
                jax.ShapeDtypeStruct((devices, out_rows, PAIR), bf16),
                jax.ShapeDtypeStruct((blocks, GATE_ROW + 16, PAIR), bf16),
            ],
            scratch_shapes=[pltpu.VMEM((8, PAIR), f32)],
            compiler_params=params,
            name="attend",
        )(arrived, text_rows, gains, gates)
        backs.append(lax.all_to_all(back, ("blk", "uly"), 0, 0, tiled=True))
    pays = lax.all_to_all(pay, "blk", 0, 0, tiled=True)

    tq_grad, tk_grad, tv_grad, txt_gate_grad, gate_rows = pl.pallas_call(
        functools.partial(text_kernel, half_heads),
        in_specs=[vmem],
        out_specs=[vmem] * 5,
        out_shape=[jax.ShapeDtypeStruct((txt, half_width), bf16)] * 3
        + [
            jax.ShapeDtypeStruct((1, half_width), f32),
            jax.ShapeDtypeStruct((samples, 1, half_width), f32),
        ],
        compiler_params=params,
        name="text",
    )(pays)
    gate_all = lax.all_to_all(gate_rows, "dp", 0, 0, tiled=True).reshape(samples, half_width)
    modulation_grad = pl.pallas_call(
        modulation_kernel,
        in_specs=[vmem] * 2,
        out_specs=vmem,
        out_shape=jax.ShapeDtypeStruct((width_rows, half_width), f32),
        compiler_params=params,
        name="modulation",
    )(cond_all, gate_all)
    out_query, out_key, out_value = pl.pallas_call(
        functools.partial(unpack_kernel, half_heads, chunks),
        in_specs=[vmem] * len(backs),
        out_specs=[vmem] * 3,
        out_shape=[jax.ShapeDtypeStruct((rows, width), bf16)] * 3,
        compiler_params=params,
        name="unpack",
    )(*backs)
    return (
        out_query[None],
        out_key[None],
        out_value[None],
        tq_grad[None],
        tk_grad[None],
        tv_grad[None],
        modulation_grad,
        txt_gate_grad,
    )


def solution(mesh):
    in_specs = (
        P("dp", ("blk", "uly"), None),
        P("dp", ("blk", "uly"), None),
        P("dp", ("blk", "uly"), None),
        P("dp", ("blk", "uly"), None),
        P("dp", None, "uly"),
        P("dp", None, "uly"),
        P("dp", None, "uly"),
        P("dp", None, "uly"),
        P("dp", None),
        P("dp", None),
        P("dp", None),
        P(),
    )
    out_specs = (
        P("dp", ("blk", "uly"), None),
        P("dp", ("blk", "uly"), None),
        P("dp", ("blk", "uly"), None),
        P("dp", None, "uly"),
        P("dp", None, "uly"),
        P("dp", None, "uly"),
        P("blk", "uly"),
        P("dp", "uly"),
    )
    return jax.shard_map(shards, mesh=mesh, in_specs=in_specs, out_specs=out_specs, check_vma=False)
```

```python
import functools

import jax
import jax.numpy as jnp
from jax import lax
from jax.experimental import pallas as pl
from jax.experimental.pallas import tpu as pltpu
from jax.sharding import PartitionSpec as P

HEAD = 64
PAIR = 2 * HEAD
EPS = 1e-06
SLOTS = 5
TEXT_ROWS = 48
GATE_ROWS = 16
ROUTES = 8
CHUNKS = ((0, 1, 2), (3, 4))
VMEM = 56 * 2**20
f32 = jnp.float32
bf16 = jnp.bfloat16


def head_of(dest, slot, half_heads):
    place = (dest // 2) * SLOTS + slot
    return (dest % 2) * half_heads + place if place < half_heads else None


def matmul(left, right):
    return jnp.dot(left, right, preferred_element_type=f32)


def matmul_nt(left, right):
    return lax.dot_general(left, right, (((1,), (1,)), ((), ())), preferred_element_type=f32)


def split_two(wide):
    high = wide.astype(bf16)
    return high, (wide - high.astype(f32)).astype(bf16)


def split_three(wide):
    high = wide.astype(bf16)
    rest = wide - high.astype(f32)
    middle = rest.astype(bf16)
    return high, middle, (rest - middle.astype(f32)).astype(bf16)


def half_means(wide, averager):
    return matmul(jnp.concatenate(split_two(wide), 1), averager)


def route(place, index, way=1):
    blocks = ROUTES // 2
    return ((place // 2 + blocks + way * (index // 2)) % blocks) * 2 + (place + index) % 2


def pack_kernel(
    half_heads,
    chunks,
    place_ref,
    iq_ref,
    ik_ref,
    iv_ref,
    ic_ref,
    tq_ref,
    tk_ref,
    tv_ref,
    tc_ref,
    ig_ref,
    tg_ref,
    *out_refs,
):
    send_refs, kept_refs = out_refs[: len(chunks)], out_refs[len(chunks) :]

    def columns(ref, head):
        return ref[:, head * HEAD : (head + 1) * HEAD]

    rows = iq_ref.shape[0]
    for slots, send_ref in zip(chunks, send_refs):
        for dest in range(send_ref.shape[0]):
            for position, slot in enumerate(slots):
                head = head_of(dest, slot, half_heads)
                for pair, (first, second) in enumerate(((iq_ref, ik_ref), (iv_ref, ic_ref))):
                    tile = (
                        jnp.zeros((rows, PAIR), bf16)
                        if head is None
                        else jnp.concatenate([columns(first, head), columns(second, head)], 1)
                    )
                    start = (2 * position + pair) * rows
                    send_ref[dest, start : start + rows, :] = tile
    if not kept_refs:
        return
    text_ref, gate_ref = kept_refs
    place = place_ref[0]
    for device in range(send_refs[0].shape[0]):

        @pl.when(place == device)
        def _():
            for slot in range(SLOTS):
                head = head_of(device, slot, half_heads)
                local = None if head is None else head - (device % 2) * half_heads
                for pair, (first, second) in enumerate(((tq_ref, tk_ref), (tv_ref, tc_ref))):
                    tile = (
                        jnp.zeros((first.shape[0], PAIR), bf16)
                        if local is None
                        else jnp.concatenate([columns(first, local), columns(second, local)], 1)
                    )
                    text_ref[:, (2 * slot + pair) * PAIR : (2 * slot + pair + 1) * PAIR] = tile
                for row, ref in enumerate((ig_ref, tg_ref)):
                    gate = jnp.zeros((1, HEAD), bf16) if head is None else columns(ref, head)
                    gate = gate.astype(f32)
                    gate_ref[slot, row : row + 1, :] = jnp.concatenate([gate, gate], 1)


def attend_kernel(slots, *refs):
    first, last = slots[0] == 0, slots[-1] == SLOTS - 1
    count = len(slots)
    in_ref, text_ref, gain_ref, gate_ref, *refs = refs
    if not first:
        place_ref, earlier_pay_ref, earlier_sum_ref, *refs = refs
    if first:
        out_ref, pay_ref, sum_ref = refs
    else:
        out_refs = refs
    devices, tile_rows = in_ref.shape[0], in_ref.shape[1] // (2 * count)
    rows, txt = devices * tile_rows, text_ref.shape[0]
    total_rows = rows + txt
    row_at = lax.broadcasted_iota(jnp.int32, (2 * PAIR, PAIR), 0)
    lane_at = lax.broadcasted_iota(jnp.int32, (2 * PAIR, PAIR), 1)
    averager = jnp.where((row_at % PAIR) // HEAD == lane_at // HEAD, 1.0 / HEAD, 0.0).astype(bf16)
    ones = jnp.ones((2 * PAIR, PAIR), bf16)
    lane = lax.broadcasted_iota(jnp.int32, (total_rows, PAIR), 1)
    gain = jnp.concatenate(
        [
            jnp.broadcast_to(gain_ref[0:1, :], (rows, PAIR)),
            jnp.broadcast_to(gain_ref[1:2, :], (txt, PAIR)),
        ],
        0,
    )
    heads = range(count)

    def joint(head, pair):
        tile = 2 * head + pair
        at = slice(tile * tile_rows, (tile + 1) * tile_rows)
        if first:
            image = in_ref[:, at, :].reshape(rows, PAIR)
        else:
            order = [route(place_ref[0], index, -1) for index in range(devices)]
            image = jnp.concatenate([in_ref[device, at, :] for device in order], 0)
        place = 2 * slots[head] + pair
        return jnp.concatenate([image, text_ref[:, place * PAIR : (place + 1) * PAIR]], 0)

    raw = [joint(head, 0).astype(f32) for head in heads]
    value_cotan = [joint(head, 1) for head in heads]
    inverse = [lax.rsqrt(half_means(x * x, averager) + EPS) for x in raw]
    normed = [(x * inv * gain).astype(bf16) for x, inv in zip(raw, inverse)]
    queries = [x[:, :HEAD] for x in normed]
    keys = [x[:, HEAD:] for x in normed]
    blank = jnp.zeros((total_rows, HEAD), bf16)
    values_ones = [
        jnp.concatenate([x[:, :HEAD], jnp.ones((total_rows, HEAD), bf16)], 1) for x in value_cotan
    ]
    keys_zeros = [jnp.concatenate([x, blank], 1) for x in keys]
    cotan = [x[:, HEAD:].astype(f32) for x in value_cotan]

    def upstream_of(head):
        slot = slots[head]
        gate = jnp.concatenate(
            [
                jnp.broadcast_to(gate_ref[slot, 0:1, :HEAD], (rows, HEAD)),
                jnp.broadcast_to(gate_ref[slot, 1:2, :HEAD], (txt, HEAD)),
            ],
            0,
        )
        return (cotan[head] * gate).astype(bf16).astype(f32)

    upstream = [upstream_of(head) for head in heads]
    scores = [matmul_nt(q * jnp.asarray(0.125, bf16), k) for q, k in zip(queries, keys)]
    exponent = [jnp.exp(x).astype(bf16) for x in scores]
    weighted = [matmul(e, v) for e, v in zip(exponent, values_ones)]

    def scaled_upstream(head):
        over_total = 1.0 / weighted[head][:, HEAD:]
        attention = (weighted[head][:, :HEAD] * over_total).astype(bf16).astype(f32)
        scaled = (upstream[head] * over_total).astype(bf16)
        product = jnp.concatenate([scaled.astype(f32) * attention, blank.astype(f32)], 1)
        delta = matmul(jnp.concatenate(split_two(product), 1), ones)
        delta_high, delta_low = split_two(delta)
        extended = jnp.where(
            lane < HEAD,
            jnp.concatenate([scaled, blank], 1),
            jnp.where(
                lane == HEAD,
                -delta_high,
                jnp.where(lane == HEAD + 1, -delta_low, jnp.zeros_like(delta_low)),
            ),
        )
        gated = cotan[head] * attention
        sums = jnp.concatenate(
            [
                jnp.sum(gated[:rows], 0, keepdims=True),
                jnp.sum(gated[rows:], 0, keepdims=True),
            ],
            1,
        )
        return scaled, extended, sums

    prepared = [scaled_upstream(head) for head in heads]
    value_grad_t = [matmul(x[0].T, e) for x, e in zip(prepared, exponent)]
    prob_grad = [matmul_nt(x[1], v) for x, v in zip(prepared, values_ones)]
    score_grad = [e * x.astype(bf16) for e, x in zip(exponent, prob_grad)]
    query_grad = [matmul(x, k) for x, k in zip(score_grad, keys_zeros)]
    value_key_grad = [
        jnp.concatenate([v, matmul(q.T, x)], 0).T
        for v, q, x in zip(value_grad_t, queries, score_grad)
    ]

    half = tile_rows // 2
    text_tiles = []
    for head in heads:
        scaled = jnp.where(lane < HEAD, query_grad[head], value_key_grad[head]) * (gain * 0.125)
        mean = half_means(raw[head] * scaled, averager)
        inv = inverse[head]
        pair_grad = (inv * scaled - raw[head] * (inv * inv * inv) * mean).astype(bf16)
        value_grad = value_key_grad[head][:, :HEAD].astype(bf16)
        begin = (count + head // 2) * tile_rows
        pairs = pair_grad[:rows].reshape(devices, tile_rows, PAIR)
        tiles = value_grad[:rows].reshape(devices, tile_rows, HEAD)
        targets = [(out_ref, slice(None))] if first else [(r, i) for i, r in enumerate(out_refs)]
        for ref, device in targets:
            value = tiles[device]
            ref[..., head * tile_rows : (head + 1) * tile_rows, :] = pairs[device]
            if head % 2 == 1:
                ref[..., begin : begin + tile_rows, HEAD:] = value
            elif head < count - 1:
                ref[..., begin : begin + tile_rows, :HEAD] = value
            else:
                ref[..., begin : begin + half, :] = jnp.concatenate(
                    [value[..., :half, :], value[..., half:, :]], -1
                )
        text_grad = value_grad[rows:]
        text_tiles += [
            pair_grad[rows:],
            jnp.concatenate([text_grad[: txt // 2], text_grad[txt // 2 :]], 1),
        ]
    sums = [x[2] for x in prepared]
    if not first:
        sums = [earlier_sum_ref[slot : slot + 1, :] for slot in range(slots[0])] + sums
    if not last:
        pay_ref[...] = jnp.concatenate(text_tiles, 0)
        sum_ref[...] = jnp.concatenate(sums + [jnp.zeros((8 - len(sums), PAIR), f32)], 0)
        return
    packed = [part.astype(f32) for part in split_three(jnp.concatenate(sums, 0))]
    packed = jnp.concatenate(packed + [jnp.zeros((GATE_ROWS - 3 * SLOTS, PAIR), f32)], 0)
    pay = jnp.concatenate([earlier_pay_ref[...]] + text_tiles + [packed.astype(bf16)], 0)
    for ref in out_refs[::2]:
        ref[ref.shape[0] - pay.shape[0] :, :] = pay


def pay_of(ref):
    start = ref.shape[0] - SLOTS * TEXT_ROWS - GATE_ROWS
    packed = ref[start + SLOTS * TEXT_ROWS :, :].astype(f32)
    return start, packed[:SLOTS] + packed[SLOTS : 2 * SLOTS] + packed[2 * SLOTS : 3 * SLOTS]


def spread_kernel(half_heads, place_ref, cond_ref, *refs):
    pay_refs, out_ref = refs[:-1], refs[-1]
    blocks = len(pay_refs)
    cond = cond_ref[...].astype(f32)
    for place in range(blocks):

        @pl.when(place_ref[0] // 2 == place)
        def _():
            heads = []
            for block in range(blocks):
                used = min(SLOTS, half_heads - block * SLOTS)
                sums = pay_of(pay_refs[(block - place) % blocks])[1]
                heads += [sums[slot : slot + 1, :HEAD] for slot in range(used)]
            rows = []
            for row in (jnp.concatenate(heads, 1), cond):
                spare = jnp.zeros((1, -row.shape[1] % PAIR), f32)
                row = jnp.concatenate([row, spare], 1)
                rows += [row[:, at : at + PAIR] for at in range(0, row.shape[1], PAIR)]
            rows.append(jnp.zeros((out_ref.shape[1] - len(rows), PAIR), f32))
            tile = jnp.concatenate(rows, 0).astype(bf16)
            for dest in range(out_ref.shape[0]):
                out_ref[dest] = tile


def modulation_kernel(in_ref, out_ref, wide_ref):
    samples, tile_rows, _ = in_ref.shape
    rows, width = out_ref.shape
    wide_ref[...] = in_ref[...].astype(f32).reshape(samples * tile_rows, PAIR)

    def over_samples(start, count):
        parts = [
            wide_ref[pl.ds(start + row, samples, stride=tile_rows), :]
            for row in range(pl.cdiv(count, PAIR))
        ]
        return jnp.concatenate(parts, 1)[:, :count].astype(bf16)

    out_ref[...] = lax.dot_general(
        over_samples(pl.cdiv(width, PAIR), rows),
        over_samples(0, width),
        (((0,), (0,)), ((), ())),
        preferred_element_type=f32,
    )


def unpack_kernel(half_heads, chunks, place_ref, first_ref, *refs):
    routed_refs, outs = refs[:ROUTES], refs[ROUTES:]
    q_ref, k_ref, v_ref, tq_ref, tk_ref, tv_ref, tg_ref, held_ref = outs
    for index, ref in enumerate(routed_refs):
        held_ref[route(place_ref[0], index)] = ref[: held_ref.shape[1], :]
    back_refs = (first_ref, held_ref)
    rows = q_ref.shape[0]
    half = rows // 2
    pieces = {}
    for slots, back_ref in zip(chunks, back_refs):
        count = len(slots)
        for source in range(back_ref.shape[0]):
            for position, slot in enumerate(slots):
                head = head_of(source, slot, half_heads)
                if head is None:
                    continue
                begin = (count + position // 2) * rows
                if position % 2 == 1:
                    value = back_ref[source, begin : begin + rows, HEAD:]
                elif position < count - 1:
                    value = back_ref[source, begin : begin + rows, :HEAD]
                else:
                    folded = back_ref[source, begin : begin + half, :]
                    value = jnp.concatenate([folded[:, :HEAD], folded[:, HEAD:]], 0)
                pair = back_ref[source, position * rows : (position + 1) * rows, :]
                pieces[head] = (pair[:, :HEAD], pair[:, HEAD:], value)
    for head in range(0, 2 * half_heads, 2):
        lanes = slice(head * HEAD, (head + 2) * HEAD)
        for which, ref in enumerate((q_ref, k_ref, v_ref)):
            ref[:, lanes] = jnp.concatenate([pieces[head][which], pieces[head + 1][which]], 1)

    txt = tq_ref.shape[0]
    pay_refs = routed_refs[::2]

    def place_text(block, pay_ref):
        start, sums = pay_of(pay_ref)
        for slot in range(min(SLOTS, half_heads - block * SLOTS)):
            head = block * SLOTS + slot
            lanes = slice(head * HEAD, (head + 1) * HEAD)
            base = start + slot * TEXT_ROWS
            pair = pay_ref[base : base + txt, :]
            folded = pay_ref[base + txt : base + TEXT_ROWS, :]
            tq_ref[:, lanes] = pair[:, :HEAD]
            tk_ref[:, lanes] = pair[:, HEAD:]
            tv_ref[:, lanes] = jnp.concatenate([folded[:, :HEAD], folded[:, HEAD:]], 0)
            tg_ref[:, lanes] = sums[slot : slot + 1, HEAD:]

    blocks = len(pay_refs)
    for shift in range(blocks):
        for block in range(blocks):

            @pl.when(place_ref[0] // 2 == (block - shift) % blocks)
            def _():
                place_text(block, pay_refs[shift])


def shards(
    img_query,
    img_key,
    img_value,
    img_cotangent,
    txt_query,
    txt_key,
    txt_value,
    txt_cotangent,
    img_gate,
    txt_gate,
    conditioning,
    norm_gains,
):
    _, rows, width = img_query.shape
    _, txt, half_width = txt_query.shape
    half_heads = half_width // HEAD
    blocks, halves, samples = lax.axis_size("blk"), lax.axis_size("uly"), lax.axis_size("dp")
    devices = blocks * halves
    params = pltpu.CompilerParams(vmem_limit_bytes=VMEM)
    place = lax.axis_index("blk") * halves + lax.axis_index("uly")
    vmem = pl.BlockSpec(memory_space=pltpu.VMEM)
    shape = jax.ShapeDtypeStruct

    def call(kernel, outs, operands, name, cost=None, smem=0, scratch=()):
        return pl.pallas_call(
            kernel,
            in_specs=[pl.BlockSpec(memory_space=pltpu.SMEM)] * smem + [vmem] * (len(operands) - smem),
            out_specs=[vmem] * len(outs),
            out_shape=outs,
            scratch_shapes=scratch,
            compiler_params=params,
            cost_estimate=cost,
            name=name,
        )(*operands)

    def exchange(operand, axes):
        return lax.all_to_all(operand, axes, 0, 0, tiled=True)

    image = (img_query[0], img_key[0], img_value[0], img_cotangent[0])
    text = (txt_query[0], txt_key[0], txt_value[0], txt_cotangent[0])
    operands = (place[None], *image, *text, img_gate, txt_gate)
    sends = []
    kept = None
    for slots in CHUNKS:
        outs = [shape((devices, 2 * len(slots) * rows, PAIR), bf16)]
        if kept is None:
            outs += [
                shape((txt, 2 * SLOTS * PAIR), bf16),
                shape((SLOTS, 2, PAIR), f32),
            ]
        send, *others = call(
            functools.partial(pack_kernel, half_heads, (slots,)), outs, operands, "pack", smem=1
        )
        sends.append(send)
        if kept is None:
            kept = others
    text_rows, gates = kept
    gains = norm_gains.reshape(2, PAIR)

    width_rows = width // blocks
    cond_row = lax.dynamic_slice_in_dim(
        conditioning, lax.axis_index("blk") * width_rows, width_rows, 1
    )

    received = []
    for send in sends:
        if received:
            send, received[-1] = lax.optimization_barrier((send, received[-1]))
        received.append(exchange(send, ("blk", "uly")))
    earlier = ()
    total_rows = devices * rows + txt
    for slots, arrived in zip(CHUNKS, received):
        count = len(slots)
        last = slots[-1] == SLOTS - 1
        pay_rows = (slots[-1] + 1) * TEXT_ROWS + (GATE_ROWS if last else 0)
        outs = [
            shape((devices, 3 * count * rows // 2, PAIR), bf16),
            shape((pay_rows, PAIR), bf16),
            shape((8, PAIR), f32),
        ]
        if last:
            outs = [
                shape((3 * count * rows // 2 + (0 if index % 2 else pay_rows), PAIR), bf16)
                for index in range(ROUTES)
            ]
        cost = pl.CostEstimate(
            flops=count * 12 * total_rows * total_rows * HEAD * 4,
            bytes_accessed=count * devices * rows * HEAD * 14,
            transcendentals=count * total_rows * total_rows,
        )
        back = call(
            functools.partial(attend_kernel, slots),
            outs,
            (arrived, text_rows, gains, gates, *earlier),
            "attend",
            cost,
        )
        if not last:
            earlier = (place[None], *back[1:])
            back_first = exchange(back[0], ("blk", "uly"))
    back_first, *back = lax.optimization_barrier((back_first, *back))
    routed = [back[0]]
    for index in range(1, ROUTES):
        pairs = [(device, route(device, index, -1)) for device in range(devices)]
        routed.append(lax.ppermute(back[index], ("blk", "uly"), pairs))
    routed = lax.optimization_barrier(routed)
    tile_rows = -(-(pl.cdiv(half_width, PAIR) + pl.cdiv(width_rows, PAIR)) // 16) * 16
    (gate_rows,) = call(
        functools.partial(spread_kernel, half_heads),
        [shape((samples, tile_rows, PAIR), bf16)],
        (place[None], cond_row, *routed[::2]),
        "spread",
        smem=1,
    )
    (modulation_grad,) = call(
        modulation_kernel,
        [shape((width_rows, half_width), f32)],
        (exchange(gate_rows, "dp"),),
        "modulation",
        scratch=[pltpu.VMEM((samples * tile_rows, PAIR), f32)],
    )
    out_query, out_key, out_value, tq_grad, tk_grad, tv_grad, txt_gate_grad = call(
        functools.partial(unpack_kernel, half_heads, CHUNKS),
        [shape((rows, width), bf16)] * 3
        + [shape((txt, half_width), bf16)] * 3
        + [shape((1, half_width), f32)],
        (place[None], back_first, *routed),
        "unpack",
        smem=1,
        scratch=[pltpu.VMEM((devices, 3 * len(CHUNKS[1]) * rows // 2, PAIR), bf16)],
    )
    return (
        out_query[None],
        out_key[None],
        out_value[None],
        tq_grad[None],
        tk_grad[None],
        tv_grad[None],
        modulation_grad,
        txt_gate_grad,
    )


def solution(mesh):
    in_specs = (
        P("dp", ("blk", "uly"), None),
        P("dp", ("blk", "uly"), None),
        P("dp", ("blk", "uly"), None),
        P("dp", ("blk", "uly"), None),
        P("dp", None, "uly"),
        P("dp", None, "uly"),
        P("dp", None, "uly"),
        P("dp", None, "uly"),
        P("dp", None),
        P("dp", None),
        P("dp", None),
        P(),
    )
    out_specs = (
        P("dp", ("blk", "uly"), None),
        P("dp", ("blk", "uly"), None),
        P("dp", ("blk", "uly"), None),
        P("dp", None, "uly"),
        P("dp", None, "uly"),
        P("dp", None, "uly"),
        P("blk", "uly"),
        P("dp", "uly"),
    )
    return jax.shard_map(shards, mesh=mesh, in_specs=in_specs, out_specs=out_specs, check_vma=False)
```

```python
import functools

import jax
import jax.numpy as jnp
from jax import lax
from jax.experimental import pallas as pl
from jax.experimental.pallas import tpu as pltpu
from jax.sharding import PartitionSpec as P

HEAD = 64
PAIR = 2 * HEAD
EPS = 1e-06
SLOTS = 5
TEXT_ROWS = 48
GATE_ROWS = 16
ROUTES = 8
CHUNKS = ((0, 1, 2), (3, 4))
VMEM = 56 * 2**20
f32 = jnp.float32
bf16 = jnp.bfloat16


def head_of(dest, slot, half_heads):
    place = (dest // 2) * SLOTS + slot
    return (dest % 2) * half_heads + place if place < half_heads else None


def matmul(left, right):
    return jnp.dot(left, right, preferred_element_type=f32)


def matmul_nt(left, right):
    return lax.dot_general(left, right, (((1,), (1,)), ((), ())), preferred_element_type=f32)


def split_two(wide):
    high = wide.astype(bf16)
    return high, (wide - high.astype(f32)).astype(bf16)


def split_three(wide):
    high = wide.astype(bf16)
    rest = wide - high.astype(f32)
    middle = rest.astype(bf16)
    return high, middle, (rest - middle.astype(f32)).astype(bf16)


def half_means(wide, averager):
    return matmul(jnp.concatenate(split_two(wide), 1), averager)


def route(place, index, way=1):
    blocks = ROUTES // 2
    return ((place // 2 + blocks + way * (index // 2)) % blocks) * 2 + (place + index) % 2


def pack_kernel(half_heads, slots, place_ref, iq_ref, ik_ref, iv_ref, ic_ref, *refs):
    def columns(ref, head):
        return ref[:, head * HEAD : (head + 1) * HEAD]

    rows = iq_ref.shape[0]
    if len(refs) == 1:
        (send_ref,) = refs
    else:
        tq_ref, tk_ref, tv_ref, tc_ref, ig_ref, tg_ref, send_ref, text_ref, gate_ref = refs
    for dest in range(send_ref.shape[0]):
        for position, slot in enumerate(slots):
            head = head_of(dest, slot, half_heads)
            for pair, (first, second) in enumerate(((iq_ref, ik_ref), (iv_ref, ic_ref))):
                tile = (
                    jnp.zeros((rows, PAIR), bf16)
                    if head is None
                    else jnp.concatenate([columns(first, head), columns(second, head)], 1)
                )
                start = (2 * position + pair) * rows
                send_ref[dest, start : start + rows, :] = tile
    if len(refs) == 1:
        return
    place = place_ref[0]
    for device in range(send_ref.shape[0]):

        @pl.when(place == device)
        def _():
            for slot in range(SLOTS):
                head = head_of(device, slot, half_heads)
                local = None if head is None else head - (device % 2) * half_heads
                for pair, (first, second) in enumerate(((tq_ref, tk_ref), (tv_ref, tc_ref))):
                    tile = (
                        jnp.zeros((first.shape[0], PAIR), bf16)
                        if local is None
                        else jnp.concatenate([columns(first, local), columns(second, local)], 1)
                    )
                    text_ref[:, (2 * slot + pair) * PAIR : (2 * slot + pair + 1) * PAIR] = tile
                for row, ref in enumerate((ig_ref, tg_ref)):
                    gate = jnp.zeros((1, HEAD), bf16) if head is None else columns(ref, head)
                    gate = gate.astype(f32)
                    gate_ref[slot, row : row + 1, :] = jnp.concatenate([gate, gate], 1)


def attend_kernel(slots, *refs):
    first, last = slots[0] == 0, slots[-1] == SLOTS - 1
    count = len(slots)
    in_ref, text_ref, gain_ref, gate_ref, *refs = refs
    if not first:
        place_ref, earlier_pay_ref, earlier_sum_ref, *refs = refs
    if first:
        out_ref, pay_ref, sum_ref = refs
    else:
        out_refs, sum_ref = refs[:-1], refs[-1]
    devices, tile_rows = in_ref.shape[0], in_ref.shape[1] // (2 * count)
    rows, txt = devices * tile_rows, text_ref.shape[0]
    total_rows = rows + txt
    row_at = lax.broadcasted_iota(jnp.int32, (2 * PAIR, PAIR), 0)
    lane_at = lax.broadcasted_iota(jnp.int32, (2 * PAIR, PAIR), 1)
    averager = jnp.where((row_at % PAIR) // HEAD == lane_at // HEAD, 1.0 / HEAD, 0.0).astype(bf16)
    ones = jnp.ones((2 * PAIR, PAIR), bf16)
    lane = lax.broadcasted_iota(jnp.int32, (total_rows, PAIR), 1)
    gain = jnp.concatenate(
        [
            jnp.broadcast_to(gain_ref[0:1, :], (rows, PAIR)),
            jnp.broadcast_to(gain_ref[1:2, :], (txt, PAIR)),
        ],
        0,
    )
    heads = range(count)

    def joint(head, pair):
        tile = 2 * head + pair
        at = slice(tile * tile_rows, (tile + 1) * tile_rows)
        if first:
            image = in_ref[:, at, :].reshape(rows, PAIR)
        else:
            order = [route(place_ref[0], index, -1) for index in range(devices)]
            image = jnp.concatenate([in_ref[device, at, :] for device in order], 0)
        place = 2 * slots[head] + pair
        return jnp.concatenate([image, text_ref[:, place * PAIR : (place + 1) * PAIR]], 0)

    raw = [joint(head, 0).astype(f32) for head in heads]
    value_cotan = [joint(head, 1) for head in heads]
    inverse = [lax.rsqrt(half_means(x * x, averager) + EPS) for x in raw]
    normed = [(x * inv * gain).astype(bf16) for x, inv in zip(raw, inverse)]
    queries = [x[:, :HEAD] for x in normed]
    keys = [x[:, HEAD:] for x in normed]
    blank = jnp.zeros((total_rows, HEAD), bf16)
    values_ones = [
        jnp.concatenate([x[:, :HEAD], jnp.ones((total_rows, HEAD), bf16)], 1) for x in value_cotan
    ]
    keys_zeros = [jnp.concatenate([x, blank], 1) for x in keys]
    cotan = [x[:, HEAD:].astype(f32) for x in value_cotan]

    def upstream_of(head):
        slot = slots[head]
        gate = jnp.concatenate(
            [
                jnp.broadcast_to(gate_ref[slot, 0:1, :HEAD], (rows, HEAD)),
                jnp.broadcast_to(gate_ref[slot, 1:2, :HEAD], (txt, HEAD)),
            ],
            0,
        )
        return (cotan[head] * gate).astype(bf16).astype(f32)

    upstream = [upstream_of(head) for head in heads]
    scores = [matmul_nt(q * jnp.asarray(0.125, bf16), k) for q, k in zip(queries, keys)]
    exponent = [jnp.exp(x).astype(bf16) for x in scores]
    weighted = [matmul(e, v) for e, v in zip(exponent, values_ones)]

    def scaled_upstream(head):
        over_total = 1.0 / weighted[head][:, HEAD:]
        attention = (weighted[head][:, :HEAD] * over_total).astype(bf16).astype(f32)
        scaled = (upstream[head] * over_total).astype(bf16)
        product = jnp.concatenate([scaled.astype(f32) * attention, blank.astype(f32)], 1)
        delta = matmul(jnp.concatenate(split_two(product), 1), ones)
        delta_high, delta_low = split_two(delta)
        extended = jnp.where(
            lane < HEAD,
            jnp.concatenate([scaled, blank], 1),
            jnp.where(
                lane == HEAD,
                -delta_high,
                jnp.where(lane == HEAD + 1, -delta_low, jnp.zeros_like(delta_low)),
            ),
        )
        gated = cotan[head] * attention
        sums = jnp.concatenate(
            [
                jnp.sum(gated[:rows], 0, keepdims=True),
                jnp.sum(gated[rows:], 0, keepdims=True),
            ],
            1,
        )
        return scaled, extended, sums

    prepared = [scaled_upstream(head) for head in heads]
    value_grad_t = [matmul(x[0].T, e) for x, e in zip(prepared, exponent)]
    prob_grad = [matmul_nt(x[1], v) for x, v in zip(prepared, values_ones)]
    score_grad = [e * x.astype(bf16) for e, x in zip(exponent, prob_grad)]
    query_grad = [matmul(x, k) for x, k in zip(score_grad, keys_zeros)]
    value_key_grad = [
        jnp.concatenate([v, matmul(q.T, x)], 0).T
        for v, q, x in zip(value_grad_t, queries, score_grad)
    ]

    half = tile_rows // 2
    text_tiles = []
    for head in heads:
        scaled = jnp.where(lane < HEAD, query_grad[head], value_key_grad[head]) * (gain * 0.125)
        mean = half_means(raw[head] * scaled, averager)
        inv = inverse[head]
        pair_grad = (inv * scaled - raw[head] * (inv * inv * inv) * mean).astype(bf16)
        value_grad = value_key_grad[head][:, :HEAD].astype(bf16)
        begin = (count + head // 2) * tile_rows
        pair_at = head * tile_rows
        pairs = pair_grad[:rows].reshape(devices, tile_rows, PAIR)
        tiles = value_grad[:rows].reshape(devices, tile_rows, HEAD)
        targets = [(out_ref, slice(None))] if first else [(r, i) for i, r in enumerate(out_refs)]
        for ref, device in targets:
            value = tiles[device]
            ref[..., pair_at : pair_at + tile_rows, :] = pairs[device]
            if head % 2 == 1:
                ref[..., begin : begin + tile_rows, HEAD:] = value
            elif head < count - 1:
                ref[..., begin : begin + tile_rows, :HEAD] = value
            else:
                ref[..., begin : begin + half, :] = jnp.concatenate(
                    [value[..., :half, :], value[..., half:, :]], -1
                )
        text_grad = value_grad[rows:]
        text_tiles += [
            pair_grad[rows:],
            jnp.concatenate([text_grad[: txt // 2], text_grad[txt // 2 :]], 1),
        ]
    sums = [x[2] for x in prepared]
    if not first:
        sums = [earlier_sum_ref[slot : slot + 1, :] for slot in range(slots[0])] + sums
    if not last:
        pay_ref[...] = jnp.concatenate(text_tiles, 0)
        sum_ref[...] = jnp.concatenate(sums + [jnp.zeros((8 - len(sums), PAIR), f32)], 0)
        return
    packed = [part.astype(f32) for part in split_three(jnp.concatenate(sums, 0))]
    packed = jnp.concatenate(packed + [jnp.zeros((GATE_ROWS - 3 * SLOTS, PAIR), f32)], 0)
    sum_ref[...] = packed.astype(bf16)
    pay = jnp.concatenate([earlier_pay_ref[...]] + text_tiles, 0)
    for ref in out_refs[::2]:
        ref[ref.shape[0] - pay.shape[0] :, :] = pay


def sums_of(ref):
    packed = ref[...].astype(f32)
    return packed[:SLOTS] + packed[SLOTS : 2 * SLOTS] + packed[2 * SLOTS : 3 * SLOTS]


def spread_kernel(half_heads, place_ref, cond_ref, *refs):
    sum_refs, out_ref = refs[:-1], refs[-1]
    blocks = len(sum_refs)
    cond = cond_ref[...].astype(f32)
    for place in range(blocks):

        @pl.when(place_ref[0] // 2 == place)
        def _():
            heads = []
            for block in range(blocks):
                used = min(SLOTS, half_heads - block * SLOTS)
                sums = sums_of(sum_refs[(block - place) % blocks])
                heads += [sums[slot : slot + 1, :HEAD] for slot in range(used)]
            rows = []
            for row in (jnp.concatenate(heads, 1), cond):
                spare = jnp.zeros((1, -row.shape[1] % PAIR), f32)
                row = jnp.concatenate([row, spare], 1)
                rows += [row[:, at : at + PAIR] for at in range(0, row.shape[1], PAIR)]
            rows.append(jnp.zeros((out_ref.shape[1] - len(rows), PAIR), f32))
            tile = jnp.concatenate(rows, 0).astype(bf16)
            for dest in range(out_ref.shape[0]):
                out_ref[dest] = tile


def modulation_kernel(in_ref, out_ref, wide_ref):
    samples, tile_rows, _ = in_ref.shape
    rows, width = out_ref.shape
    wide_ref[...] = in_ref[...].astype(f32).reshape(samples * tile_rows, PAIR)

    def over_samples(start, count):
        parts = [
            wide_ref[pl.ds(start + row, samples, stride=tile_rows), :]
            for row in range(pl.cdiv(count, PAIR))
        ]
        return jnp.concatenate(parts, 1)[:, :count].astype(bf16)

    out_ref[...] = lax.dot_general(
        over_samples(pl.cdiv(width, PAIR), rows),
        over_samples(0, width),
        (((0,), (0,)), ((), ())),
        preferred_element_type=f32,
    )


def unpack_kernel(half_heads, chunks, place_ref, first_ref, *refs):
    blocks = ROUTES // 2
    routed_refs, sum_refs, outs = refs[:ROUTES], refs[ROUTES : ROUTES + blocks], refs[ROUTES + blocks :]
    q_ref, k_ref, v_ref, tq_ref, tk_ref, tv_ref, tg_ref, held_ref = outs
    for index, ref in enumerate(routed_refs):
        held_ref[route(place_ref[0], index)] = ref[: held_ref.shape[1], :]
    rows = q_ref.shape[0]
    half = rows // 2
    pieces = {}
    for slots, back_ref in zip(chunks, (first_ref, held_ref)):
        count = len(slots)
        for source in range(back_ref.shape[0]):
            for position, slot in enumerate(slots):
                head = head_of(source, slot, half_heads)
                if head is None:
                    continue
                begin = (count + position // 2) * rows
                if position % 2 == 1:
                    value = back_ref[source, begin : begin + rows, HEAD:]
                elif position < count - 1:
                    value = back_ref[source, begin : begin + rows, :HEAD]
                else:
                    folded = back_ref[source, begin : begin + half, :]
                    value = jnp.concatenate([folded[:, :HEAD], folded[:, HEAD:]], 0)
                pair = back_ref[source, position * rows : (position + 1) * rows, :]
                pieces[head] = (pair[:, :HEAD], pair[:, HEAD:], value)
    for head in range(0, 2 * half_heads, 2):
        lanes = slice(head * HEAD, (head + 2) * HEAD)
        for which, ref in enumerate((q_ref, k_ref, v_ref)):
            ref[:, lanes] = jnp.concatenate([pieces[head][which], pieces[head + 1][which]], 1)

    txt = tq_ref.shape[0]
    pay_refs = routed_refs[::2]

    def place_text(block, pay_ref, sum_ref):
        start, sums = held_ref.shape[1], sums_of(sum_ref)
        for slot in range(min(SLOTS, half_heads - block * SLOTS)):
            head = block * SLOTS + slot
            lanes = slice(head * HEAD, (head + 1) * HEAD)
            base = start + slot * TEXT_ROWS
            pair = pay_ref[base : base + txt, :]
            folded = pay_ref[base + txt : base + TEXT_ROWS, :]
            tq_ref[:, lanes] = pair[:, :HEAD]
            tk_ref[:, lanes] = pair[:, HEAD:]
            tv_ref[:, lanes] = jnp.concatenate([folded[:, :HEAD], folded[:, HEAD:]], 0)
            tg_ref[:, lanes] = sums[slot : slot + 1, HEAD:]

    for shift in range(blocks):
        for block in range(blocks):

            @pl.when(place_ref[0] // 2 == (block - shift) % blocks)
            def _():
                place_text(block, pay_refs[shift], sum_refs[shift])


def shards(
    img_query,
    img_key,
    img_value,
    img_cotangent,
    txt_query,
    txt_key,
    txt_value,
    txt_cotangent,
    img_gate,
    txt_gate,
    conditioning,
    norm_gains,
):
    _, rows, width = img_query.shape
    _, txt, half_width = txt_query.shape
    half_heads = half_width // HEAD
    blocks, halves, samples = lax.axis_size("blk"), lax.axis_size("uly"), lax.axis_size("dp")
    devices = blocks * halves
    params = pltpu.CompilerParams(vmem_limit_bytes=VMEM)
    place = lax.axis_index("blk") * halves + lax.axis_index("uly")
    vmem = pl.BlockSpec(memory_space=pltpu.VMEM)
    shape = jax.ShapeDtypeStruct

    def call(kernel, outs, operands, name, cost=None, smem=0, scratch=()):
        return pl.pallas_call(
            kernel,
            in_specs=[pl.BlockSpec(memory_space=pltpu.SMEM)] * smem + [vmem] * (len(operands) - smem),
            out_specs=[vmem] * len(outs),
            out_shape=outs,
            scratch_shapes=scratch,
            compiler_params=params,
            cost_estimate=cost,
            name=name,
        )(*operands)

    def exchange(operand, axes):
        return lax.all_to_all(operand, axes, 0, 0, tiled=True)

    image = (img_query[0], img_key[0], img_value[0], img_cotangent[0])
    text = (txt_query[0], txt_key[0], txt_value[0], txt_cotangent[0])
    sends = []
    for slots in CHUNKS:
        outs = [shape((devices, 2 * len(slots) * rows, PAIR), bf16)]
        if slots[-1] == SLOTS - 1:
            outs += [
                shape((txt, 2 * SLOTS * PAIR), bf16),
                shape((SLOTS, 2, PAIR), f32),
            ]
            operands = (*image, *text, img_gate, txt_gate)
        else:
            operands = image
        send, *kept = call(
            functools.partial(pack_kernel, half_heads, slots),
            outs,
            (place[None], *operands),
            "pack",
            smem=1,
        )
        sends.append(send)
    text_rows, gates = kept
    gains = norm_gains.reshape(2, PAIR)

    width_rows = width // blocks
    cond_row = lax.dynamic_slice_in_dim(
        conditioning, lax.axis_index("blk") * width_rows, width_rows, 1
    )

    received = []
    for send in sends:
        if received:
            send, received[-1] = lax.optimization_barrier((send, received[-1]))
        received.append(exchange(send, ("blk", "uly")))
    earlier = ()
    total_rows = devices * rows + txt
    for slots, arrived in zip(CHUNKS, received):
        count = len(slots)
        last = slots[-1] == SLOTS - 1
        pay_rows = (slots[-1] + 1) * TEXT_ROWS
        outs = [
            shape((devices, 3 * count * rows // 2, PAIR), bf16),
            shape((pay_rows, PAIR), bf16),
            shape((8, PAIR), f32),
        ]
        if last:
            outs = [
                shape((3 * count * rows // 2 + (0 if index % 2 else pay_rows), PAIR), bf16)
                for index in range(ROUTES)
            ] + [shape((GATE_ROWS, PAIR), bf16)]
        cost = pl.CostEstimate(
            flops=count * 12 * total_rows * total_rows * HEAD * 4,
            bytes_accessed=count * devices * rows * HEAD * 14,
            transcendentals=count * total_rows * total_rows,
        )
        back = call(
            functools.partial(attend_kernel, slots),
            outs,
            (arrived, text_rows, gains, gates, *earlier),
            "attend",
            cost,
        )
        if not last:
            earlier = (place[None], *back[1:])
            back_first = exchange(back[0], ("blk", "uly"))
    *back, own_sums = back

    def step_back(operand, index):
        pairs = [(device, route(device, index, -1)) for device in range(devices)]
        return lax.ppermute(operand, ("blk", "uly"), pairs)

    sums = [own_sums] + [step_back(own_sums, index) for index in range(2, ROUTES, 2)]
    *back, sums = lax.optimization_barrier((*back, sums))
    routed = [back[0]] + [step_back(back[index], index) for index in range(1, ROUTES)]
    tile_rows = -(-(pl.cdiv(half_width, PAIR) + pl.cdiv(width_rows, PAIR)) // 16) * 16
    (gate_rows,) = call(
        functools.partial(spread_kernel, half_heads),
        [shape((samples, tile_rows, PAIR), bf16)],
        (place[None], cond_row, *sums),
        "spread",
        smem=1,
    )
    gate_rows, back_first = lax.optimization_barrier((gate_rows, back_first))
    gate_all = exchange(gate_rows, "dp")
    (modulation_grad,) = call(
        modulation_kernel,
        [shape((width_rows, half_width), f32)],
        (gate_all,),
        "modulation",
        scratch=[pltpu.VMEM((samples * tile_rows, PAIR), f32)],
    )
    modulation_grad, *routed = lax.optimization_barrier((modulation_grad, *routed))
    out_query, out_key, out_value, tq_grad, tk_grad, tv_grad, txt_gate_grad = call(
        functools.partial(unpack_kernel, half_heads, CHUNKS),
        [shape((rows, width), bf16)] * 3
        + [shape((txt, half_width), bf16)] * 3
        + [shape((1, half_width), f32)],
        (place[None], back_first, *routed, *sums),
        "unpack",
        smem=1,
        scratch=[pltpu.VMEM((devices, 3 * len(CHUNKS[1]) * rows // 2, PAIR), bf16)],
    )
    return (
        out_query[None],
        out_key[None],
        out_value[None],
        tq_grad[None],
        tk_grad[None],
        tv_grad[None],
        modulation_grad,
        txt_gate_grad,
    )


def solution(mesh):
    in_specs = (
        P("dp", ("blk", "uly"), None),
        P("dp", ("blk", "uly"), None),
        P("dp", ("blk", "uly"), None),
        P("dp", ("blk", "uly"), None),
        P("dp", None, "uly"),
        P("dp", None, "uly"),
        P("dp", None, "uly"),
        P("dp", None, "uly"),
        P("dp", None),
        P("dp", None),
        P("dp", None),
        P(),
    )
    out_specs = (
        P("dp", ("blk", "uly"), None),
        P("dp", ("blk", "uly"), None),
        P("dp", ("blk", "uly"), None),
        P("dp", None, "uly"),
        P("dp", None, "uly"),
        P("dp", None, "uly"),
        P("blk", "uly"),
        P("dp", "uly"),
    )
    return jax.shard_map(shards, mesh=mesh, in_specs=in_specs, out_specs=out_specs, check_vma=False)
```

```python
import functools

import jax
import jax.numpy as jnp
from jax import lax
from jax.experimental import pallas as pl
from jax.experimental.pallas import tpu as pltpu
from jax.sharding import PartitionSpec as P

HEAD = 64
PAIR = 2 * HEAD
EPS = 1e-06
SLOTS = 5
TEXT_ROWS = 48
GATE_ROWS = 16
ROUTES = 8
CHUNKS = ((0, 1, 2), (3, 4))
VMEM = 56 * 2**20
f32 = jnp.float32
bf16 = jnp.bfloat16


def head_of(dest, slot, half_heads):
    place = (dest // 2) * SLOTS + slot
    return (dest % 2) * half_heads + place if place < half_heads else None


def matmul(left, right):
    return jnp.dot(left, right, preferred_element_type=f32)


def matmul_nt(left, right):
    return lax.dot_general(left, right, (((1,), (1,)), ((), ())), preferred_element_type=f32)


def split_two(wide):
    high = wide.astype(bf16)
    return high, (wide - high.astype(f32)).astype(bf16)


def split_three(wide):
    high = wide.astype(bf16)
    rest = wide - high.astype(f32)
    middle = rest.astype(bf16)
    return high, middle, (rest - middle.astype(f32)).astype(bf16)


def half_means(wide, averager):
    return matmul(jnp.concatenate(split_two(wide), 1), averager)


def route(place, index, way=1):
    blocks = ROUTES // 2
    shift = (index // 2 + blocks // 2 * (index % 2)) % blocks
    return ((place // 2 + blocks + way * shift) % blocks) * 2 + (place + index) % 2


def pack_kernel(half_heads, slots, place_ref, iq_ref, ik_ref, iv_ref, ic_ref, *refs):
    def columns(ref, head):
        return ref[:, head * HEAD : (head + 1) * HEAD]

    rows = iq_ref.shape[0]
    if len(refs) == 1:
        (send_ref,) = refs
    else:
        tq_ref, tk_ref, tv_ref, tc_ref, ig_ref, tg_ref, send_ref, text_ref, gate_ref = refs
    for dest in range(send_ref.shape[0]):
        for position, slot in enumerate(slots):
            head = head_of(dest, slot, half_heads)
            for pair, (first, second) in enumerate(((iq_ref, ik_ref), (iv_ref, ic_ref))):
                tile = (
                    jnp.zeros((rows, PAIR), bf16)
                    if head is None
                    else jnp.concatenate([columns(first, head), columns(second, head)], 1)
                )
                start = (2 * position + pair) * rows
                send_ref[dest, start : start + rows, :] = tile
    if len(refs) == 1:
        return
    place = place_ref[0]
    for device in range(send_ref.shape[0]):

        @pl.when(place == device)
        def _():
            for slot in range(SLOTS):
                head = head_of(device, slot, half_heads)
                local = None if head is None else head - (device % 2) * half_heads
                for pair, (first, second) in enumerate(((tq_ref, tk_ref), (tv_ref, tc_ref))):
                    tile = (
                        jnp.zeros((first.shape[0], PAIR), bf16)
                        if local is None
                        else jnp.concatenate([columns(first, local), columns(second, local)], 1)
                    )
                    text_ref[:, (2 * slot + pair) * PAIR : (2 * slot + pair + 1) * PAIR] = tile
                for row, ref in enumerate((ig_ref, tg_ref)):
                    gate = jnp.zeros((1, HEAD), bf16) if head is None else columns(ref, head)
                    gate = gate.astype(f32)
                    gate_ref[slot, row : row + 1, :] = jnp.concatenate([gate, gate], 1)


def attend_kernel(slots, *refs):
    first, last = slots[0] == 0, slots[-1] == SLOTS - 1
    count = len(slots)
    in_ref, text_ref, gain_ref, gate_ref, *refs = refs
    if not first:
        place_ref, earlier_pay_ref, earlier_sum_ref, *refs = refs
    if first:
        out_ref, pay_ref, sum_ref = refs
    else:
        out_refs, sum_ref = refs[:-1], refs[-1]
    devices, tile_rows = in_ref.shape[0], in_ref.shape[1] // (2 * count)
    rows, txt = devices * tile_rows, text_ref.shape[0]
    total_rows = rows + txt
    row_at = lax.broadcasted_iota(jnp.int32, (2 * PAIR, PAIR), 0)
    lane_at = lax.broadcasted_iota(jnp.int32, (2 * PAIR, PAIR), 1)
    averager = jnp.where((row_at % PAIR) // HEAD == lane_at // HEAD, 1.0 / HEAD, 0.0).astype(bf16)
    ones = jnp.ones((2 * PAIR, PAIR), bf16)
    lane = lax.broadcasted_iota(jnp.int32, (total_rows, PAIR), 1)
    gain = jnp.concatenate(
        [
            jnp.broadcast_to(gain_ref[0:1, :], (rows, PAIR)),
            jnp.broadcast_to(gain_ref[1:2, :], (txt, PAIR)),
        ],
        0,
    )
    heads = range(count)

    def joint(head, pair):
        tile = 2 * head + pair
        at = slice(tile * tile_rows, (tile + 1) * tile_rows)
        if first:
            image = in_ref[:, at, :].reshape(rows, PAIR)
        else:
            order = [route(place_ref[0], index, -1) for index in range(devices)]
            image = jnp.concatenate([in_ref[device, at, :] for device in order], 0)
        place = 2 * slots[head] + pair
        return jnp.concatenate([image, text_ref[:, place * PAIR : (place + 1) * PAIR]], 0)

    raw = [joint(head, 0).astype(f32) for head in heads]
    value_cotan = [joint(head, 1) for head in heads]
    inverse = [lax.rsqrt(half_means(x * x, averager) + EPS) for x in raw]
    normed = [(x * inv * gain).astype(bf16) for x, inv in zip(raw, inverse)]
    queries = [x[:, :HEAD] for x in normed]
    keys = [x[:, HEAD:] for x in normed]
    blank = jnp.zeros((total_rows, HEAD), bf16)
    values_ones = [
        jnp.concatenate([x[:, :HEAD], jnp.ones((total_rows, HEAD), bf16)], 1) for x in value_cotan
    ]
    keys_zeros = [jnp.concatenate([x, blank], 1) for x in keys]
    cotan = [x[:, HEAD:].astype(f32) for x in value_cotan]

    def upstream_of(head):
        slot = slots[head]
        gate = jnp.concatenate(
            [
                jnp.broadcast_to(gate_ref[slot, 0:1, :HEAD], (rows, HEAD)),
                jnp.broadcast_to(gate_ref[slot, 1:2, :HEAD], (txt, HEAD)),
            ],
            0,
        )
        return (cotan[head] * gate).astype(bf16).astype(f32)

    upstream = [upstream_of(head) for head in heads]
    scores = [matmul_nt(q * jnp.asarray(0.125, bf16), k) for q, k in zip(queries, keys)]
    exponent = [jnp.exp(x).astype(bf16) for x in scores]
    weighted = [matmul(e, v) for e, v in zip(exponent, values_ones)]

    def scaled_upstream(head):
        over_total = 1.0 / weighted[head][:, HEAD:]
        attention = (weighted[head][:, :HEAD] * over_total).astype(bf16).astype(f32)
        scaled = (upstream[head] * over_total).astype(bf16)
        product = jnp.concatenate([scaled.astype(f32) * attention, blank.astype(f32)], 1)
        delta = matmul(jnp.concatenate(split_two(product), 1), ones)
        delta_high, delta_low = split_two(delta)
        extended = jnp.where(
            lane < HEAD,
            jnp.concatenate([scaled, blank], 1),
            jnp.where(
                lane == HEAD,
                -delta_high,
                jnp.where(lane == HEAD + 1, -delta_low, jnp.zeros_like(delta_low)),
            ),
        )
        gated = cotan[head] * attention
        sums = jnp.concatenate(
            [
                jnp.sum(gated[:rows], 0, keepdims=True),
                jnp.sum(gated[rows:], 0, keepdims=True),
            ],
            1,
        )
        return scaled, extended, sums

    prepared = [scaled_upstream(head) for head in heads]
    value_grad_t = [matmul(x[0].T, e) for x, e in zip(prepared, exponent)]
    prob_grad = [matmul_nt(x[1], v) for x, v in zip(prepared, values_ones)]
    score_grad = [e * x.astype(bf16) for e, x in zip(exponent, prob_grad)]
    query_grad = [matmul(x, k) for x, k in zip(score_grad, keys_zeros)]
    value_key_grad = [
        jnp.concatenate([v, matmul(q.T, x)], 0).T
        for v, q, x in zip(value_grad_t, queries, score_grad)
    ]

    half = tile_rows // 2
    text_tiles = []
    for head in heads:
        scaled = jnp.where(lane < HEAD, query_grad[head], value_key_grad[head]) * (gain * 0.125)
        mean = half_means(raw[head] * scaled, averager)
        inv = inverse[head]
        pair_grad = (inv * scaled - raw[head] * (inv * inv * inv) * mean).astype(bf16)
        value_grad = value_key_grad[head][:, :HEAD].astype(bf16)
        begin = (count + head // 2) * tile_rows
        pair_at = head * tile_rows
        pairs = pair_grad[:rows].reshape(devices, tile_rows, PAIR)
        tiles = value_grad[:rows].reshape(devices, tile_rows, HEAD)
        targets = [(out_ref, slice(None))] if first else [(r, i) for i, r in enumerate(out_refs)]
        for ref, device in targets:
            value = tiles[device]
            ref[..., pair_at : pair_at + tile_rows, :] = pairs[device]
            if head % 2 == 1:
                ref[..., begin : begin + tile_rows, HEAD:] = value
            elif head < count - 1:
                ref[..., begin : begin + tile_rows, :HEAD] = value
            else:
                ref[..., begin : begin + half, :] = jnp.concatenate(
                    [value[..., :half, :], value[..., half:, :]], -1
                )
        text_grad = value_grad[rows:]
        text_tiles += [
            pair_grad[rows:],
            jnp.concatenate([text_grad[: txt // 2], text_grad[txt // 2 :]], 1),
        ]
    sums = [x[2] for x in prepared]
    if not first:
        sums = [earlier_sum_ref[slot : slot + 1, :] for slot in range(slots[0])] + sums
    if not last:
        pay_ref[...] = jnp.concatenate(text_tiles, 0)
        sum_ref[...] = jnp.concatenate(sums + [jnp.zeros((8 - len(sums), PAIR), f32)], 0)
        return
    packed = [part.astype(f32) for part in split_three(jnp.concatenate(sums, 0))]
    packed = jnp.concatenate(packed + [jnp.zeros((GATE_ROWS - 3 * SLOTS, PAIR), f32)], 0)
    sum_ref[...] = packed.astype(bf16)
    pay = jnp.concatenate([earlier_pay_ref[...]] + text_tiles, 0)
    for ref in out_refs[::2]:
        ref[ref.shape[0] - pay.shape[0] :, :] = pay


def sums_of(ref):
    packed = ref[...].astype(f32)
    return packed[:SLOTS] + packed[SLOTS : 2 * SLOTS] + packed[2 * SLOTS : 3 * SLOTS]


def spread_kernel(half_heads, place_ref, cond_ref, *refs):
    sum_refs, out_ref = refs[:-1], refs[-1]
    blocks = len(sum_refs)
    cond = cond_ref[...].astype(f32)
    for place in range(blocks):

        @pl.when(place_ref[0] // 2 == place)
        def _():
            heads = []
            for block in range(blocks):
                used = min(SLOTS, half_heads - block * SLOTS)
                sums = sums_of(sum_refs[(block - place) % blocks])
                heads += [sums[slot : slot + 1, :HEAD] for slot in range(used)]
            rows = []
            for row in (jnp.concatenate(heads, 1), cond):
                spare = jnp.zeros((1, -row.shape[1] % PAIR), f32)
                row = jnp.concatenate([row, spare], 1)
                rows += [row[:, at : at + PAIR] for at in range(0, row.shape[1], PAIR)]
            rows.append(jnp.zeros((out_ref.shape[1] - len(rows), PAIR), f32))
            tile = jnp.concatenate(rows, 0).astype(bf16)
            for dest in range(out_ref.shape[0]):
                out_ref[dest] = tile


def modulation_kernel(in_ref, out_ref, wide_ref):
    samples, tile_rows, _ = in_ref.shape
    rows, width = out_ref.shape
    wide_ref[...] = in_ref[...].astype(f32).reshape(samples * tile_rows, PAIR)

    def over_samples(start, count):
        parts = [
            wide_ref[pl.ds(start + row, samples, stride=tile_rows), :]
            for row in range(pl.cdiv(count, PAIR))
        ]
        return jnp.concatenate(parts, 1)[:, :count].astype(bf16)

    out_ref[...] = lax.dot_general(
        over_samples(pl.cdiv(width, PAIR), rows),
        over_samples(0, width),
        (((0,), (0,)), ((), ())),
        preferred_element_type=f32,
    )


def unpack_kernel(half_heads, chunks, place_ref, first_ref, *refs):
    blocks = ROUTES // 2
    routed_refs, sum_refs, outs = refs[:ROUTES], refs[ROUTES : ROUTES + blocks], refs[ROUTES + blocks :]
    q_ref, k_ref, v_ref, tq_ref, tk_ref, tv_ref, tg_ref, held_ref = outs
    for index, ref in enumerate(routed_refs):
        held_ref[route(place_ref[0], index)] = ref[: held_ref.shape[1], :]
    rows = q_ref.shape[0]
    half = rows // 2
    pieces = {}
    for slots, back_ref in zip(chunks, (first_ref, held_ref)):
        count = len(slots)
        for source in range(back_ref.shape[0]):
            for position, slot in enumerate(slots):
                head = head_of(source, slot, half_heads)
                if head is None:
                    continue
                begin = (count + position // 2) * rows
                if position % 2 == 1:
                    value = back_ref[source, begin : begin + rows, HEAD:]
                elif position < count - 1:
                    value = back_ref[source, begin : begin + rows, :HEAD]
                else:
                    folded = back_ref[source, begin : begin + half, :]
                    value = jnp.concatenate([folded[:, :HEAD], folded[:, HEAD:]], 0)
                pair = back_ref[source, position * rows : (position + 1) * rows, :]
                pieces[head] = (pair[:, :HEAD], pair[:, HEAD:], value)
    for head in range(0, 2 * half_heads, 2):
        lanes = slice(head * HEAD, (head + 2) * HEAD)
        for which, ref in enumerate((q_ref, k_ref, v_ref)):
            ref[:, lanes] = jnp.concatenate([pieces[head][which], pieces[head + 1][which]], 1)

    txt = tq_ref.shape[0]
    pay_refs = routed_refs[::2]

    def place_text(block, pay_ref, sum_ref):
        start, sums = held_ref.shape[1], sums_of(sum_ref)
        for slot in range(min(SLOTS, half_heads - block * SLOTS)):
            head = block * SLOTS + slot
            lanes = slice(head * HEAD, (head + 1) * HEAD)
            base = start + slot * TEXT_ROWS
            pair = pay_ref[base : base + txt, :]
            folded = pay_ref[base + txt : base + TEXT_ROWS, :]
            tq_ref[:, lanes] = pair[:, :HEAD]
            tk_ref[:, lanes] = pair[:, HEAD:]
            tv_ref[:, lanes] = jnp.concatenate([folded[:, :HEAD], folded[:, HEAD:]], 0)
            tg_ref[:, lanes] = sums[slot : slot + 1, HEAD:]

    for shift in range(blocks):
        for block in range(blocks):

            @pl.when(place_ref[0] // 2 == (block - shift) % blocks)
            def _():
                place_text(block, pay_refs[shift], sum_refs[shift])


def shards(
    img_query,
    img_key,
    img_value,
    img_cotangent,
    txt_query,
    txt_key,
    txt_value,
    txt_cotangent,
    img_gate,
    txt_gate,
    conditioning,
    norm_gains,
):
    _, rows, width = img_query.shape
    _, txt, half_width = txt_query.shape
    half_heads = half_width // HEAD
    blocks, halves, samples = lax.axis_size("blk"), lax.axis_size("uly"), lax.axis_size("dp")
    devices = blocks * halves
    params = pltpu.CompilerParams(vmem_limit_bytes=VMEM)
    place = lax.axis_index("blk") * halves + lax.axis_index("uly")
    vmem = pl.BlockSpec(memory_space=pltpu.VMEM)
    shape = jax.ShapeDtypeStruct

    def call(kernel, outs, operands, name, cost=None, smem=0, scratch=()):
        return pl.pallas_call(
            kernel,
            in_specs=[pl.BlockSpec(memory_space=pltpu.SMEM)] * smem + [vmem] * (len(operands) - smem),
            out_specs=[vmem] * len(outs),
            out_shape=outs,
            scratch_shapes=scratch,
            compiler_params=params,
            cost_estimate=cost,
            name=name,
        )(*operands)

    def exchange(operand, axes):
        return lax.all_to_all(operand, axes, 0, 0, tiled=True)

    image = (img_query[0], img_key[0], img_value[0], img_cotangent[0])
    text = (txt_query[0], txt_key[0], txt_value[0], txt_cotangent[0])
    sends = []
    for slots in CHUNKS:
        outs = [shape((devices, 2 * len(slots) * rows, PAIR), bf16)]
        if slots[-1] == SLOTS - 1:
            outs += [
                shape((txt, 2 * SLOTS * PAIR), bf16),
                shape((SLOTS, 2, PAIR), f32),
            ]
            operands = (*image, *text, img_gate, txt_gate)
        else:
            operands = image
        send, *kept = call(
            functools.partial(pack_kernel, half_heads, slots),
            outs,
            (place[None], *operands),
            "pack",
            smem=1,
        )
        sends.append(send)
    text_rows, gates = kept
    gains = norm_gains.reshape(2, PAIR)

    width_rows = width // blocks
    cond_row = lax.dynamic_slice_in_dim(
        conditioning, lax.axis_index("blk") * width_rows, width_rows, 1
    )

    received = []
    for send in sends:
        if received:
            send, received[-1] = lax.optimization_barrier((send, received[-1]))
        received.append(exchange(send, ("blk", "uly")))
    earlier = ()
    total_rows = devices * rows + txt
    for slots, arrived in zip(CHUNKS, received):
        count = len(slots)
        last = slots[-1] == SLOTS - 1
        pay_rows = (slots[-1] + 1) * TEXT_ROWS
        outs = [
            shape((devices, 3 * count * rows // 2, PAIR), bf16),
            shape((pay_rows, PAIR), bf16),
            shape((8, PAIR), f32),
        ]
        if last:
            outs = [
                shape((3 * count * rows // 2 + (0 if index % 2 else pay_rows), PAIR), bf16)
                for index in range(ROUTES)
            ] + [shape((GATE_ROWS, PAIR), bf16)]
        cost = pl.CostEstimate(
            flops=count * 12 * total_rows * total_rows * HEAD * 4,
            bytes_accessed=count * devices * rows * HEAD * 14,
            transcendentals=count * total_rows * total_rows,
        )
        back = call(
            functools.partial(attend_kernel, slots),
            outs,
            (arrived, text_rows, gains, gates, *earlier),
            "attend",
            cost,
        )
        if not last:
            earlier = (place[None], *back[1:])
            back_first = exchange(back[0], ("blk", "uly"))
    *back, own_sums = back

    def step_back(operand, index):
        pairs = [(device, route(device, index, -1)) for device in range(devices)]
        return lax.ppermute(operand, ("blk", "uly"), pairs)

    sums = [own_sums] + [step_back(own_sums, index) for index in range(2, ROUTES, 2)]
    *back, sums = lax.optimization_barrier((*back, sums))
    routed = [back[0]] + [step_back(back[index], index) for index in range(1, ROUTES)]
    tile_rows = -(-(pl.cdiv(half_width, PAIR) + pl.cdiv(width_rows, PAIR)) // 16) * 16
    (gate_rows,) = call(
        functools.partial(spread_kernel, half_heads),
        [shape((samples, tile_rows, PAIR), bf16)],
        (place[None], cond_row, *sums),
        "spread",
        smem=1,
    )
    gate_rows, back_first = lax.optimization_barrier((gate_rows, back_first))
    gate_all = exchange(gate_rows, "dp")
    (modulation_grad,) = call(
        modulation_kernel,
        [shape((width_rows, half_width), f32)],
        (gate_all,),
        "modulation",
        scratch=[pltpu.VMEM((samples * tile_rows, PAIR), f32)],
    )
    modulation_grad, *routed = lax.optimization_barrier((modulation_grad, *routed))
    out_query, out_key, out_value, tq_grad, tk_grad, tv_grad, txt_gate_grad = call(
        functools.partial(unpack_kernel, half_heads, CHUNKS),
        [shape((rows, width), bf16)] * 3
        + [shape((txt, half_width), bf16)] * 3
        + [shape((1, half_width), f32)],
        (place[None], back_first, *routed, *sums),
        "unpack",
        smem=1,
        scratch=[pltpu.VMEM((devices, 3 * len(CHUNKS[1]) * rows // 2, PAIR), bf16)],
    )
    return (
        out_query[None],
        out_key[None],
        out_value[None],
        tq_grad[None],
        tk_grad[None],
        tv_grad[None],
        modulation_grad,
        txt_gate_grad,
    )


def solution(mesh):
    in_specs = (
        P("dp", ("blk", "uly"), None),
        P("dp", ("blk", "uly"), None),
        P("dp", ("blk", "uly"), None),
        P("dp", ("blk", "uly"), None),
        P("dp", None, "uly"),
        P("dp", None, "uly"),
        P("dp", None, "uly"),
        P("dp", None, "uly"),
        P("dp", None),
        P("dp", None),
        P("dp", None),
        P(),
    )
    out_specs = (
        P("dp", ("blk", "uly"), None),
        P("dp", ("blk", "uly"), None),
        P("dp", ("blk", "uly"), None),
        P("dp", None, "uly"),
        P("dp", None, "uly"),
        P("dp", None, "uly"),
        P("blk", "uly"),
        P("dp", "uly"),
    )
    return jax.shard_map(shards, mesh=mesh, in_specs=in_specs, out_specs=out_specs, check_vma=False)
```
